32 devices in a mesh: half: 2 (over y), row: 4 (over z), col: 4 (over x, core).
Axes of the slice: x: 2, y: 2, z: 4, core: 2. Of those that a mesh axis runs over, the one named last changes fastest.
Arguments:
- child_block: bfloat16 [2, 4, 4, 256, 4, 4, 256], P('half', None, 'row', None, None, 'col'), may hold values from -6 to 6
- child_row: bfloat16 [2, 256, 4, 4, 256], P('half', 'row', None, 'col'), may hold values from -6 to 6
- child_col: bfloat16 [2, 256, 4, 4, 256], P('half', 'col', None, 'row'), may hold values from -0.375 to 0.375
- child_pivot_inv: bfloat16 [2, 256, 256], P('half'), may hold values from -0.375 to 0.375
- child_map: int32 [2, 16], replicated, may hold values from 0 to 30, as said below
- parent_row: bfloat16 [256, 4, 8, 256], P('row', None, ('half', 'col')), may hold values from -6 to 6
- parent_col: bfloat16 [256, 8, 4, 256], P(('half', 'col'), None, 'row'), may hold values from -0.375 to 0.375
- parent_pivot_inv: bfloat16 [256, 256], replicated, may hold values from -0.375 to 0.375
- parent_diag: float32 [8, 4, 256], P(None, 'row'), may hold values from 1 to 3
Outputs:
- schur: bfloat16 [8, 4, 256, 4, 8, 256], P(None, 'row', None, None, ('half', 'col'))
The draws below stay inside these ranges and needn't reach their ends.
Inputs may be any that keep to these rules, and one draw needn't show every extreme that they name: child_map[h, 4 * k + r] = 2 * 4 * k + r + p_h[k] for k and r from 0 to 3, where p_0 and p_1 are permutations of 0 to 3.
All inputs are finite; a program needn't handle non-finite values.
Results may differ from the reference program's by a relative error of at most 0.0041.
The reference program's roundings to bfloat16 on the way count: a program that leaves them out, or rounds other values in their place, can miss the bound.
Values may be sent and summed in bfloat16 or wider, within the bound.
No kernel may reach another device: no remote copies, remote signals or barrier semaphores. Data moves between devices by JAX's collectives and lax.ppermute only.
A program may use at most 384 MiB of HBM per device.

```python
import jax
import jax.numpy as jnp
from jax import lax

TILE = 256
GRID = 4
CB_TILES = 16
PARENT_TILES = 32


def draw_child_map(key, part):
    mapped = []
    for sibling in range(2):
        shuffled = jax.random.permutation(jax.random.fold_in(key, 17 + sibling), GRID).astype(jnp.int32)
        blocks = jnp.arange(GRID, dtype=jnp.int32)
        offsets = 2 * GRID * blocks + shuffled
        mapped.append((offsets[:, None] + blocks[None, :]).reshape(-1))
    return jnp.stack(mapped).astype(jnp.int32)


def levels(stream_key, shape, split, low, high):
    def one(position, shards_of):
        heights = jax.random.uniform(jax.random.fold_in(jax.random.fold_in(stream_key, 6), position), (shards_of,), jnp.float32, low / len(split), high / len(split))
        return jnp.repeat(jnp.exp(heights), shape[position] // shards_of).reshape((-1,) + (1,) * (len(shape) - position - 1))

    gain = one(*split[0])
    for cut in split[1:]:
        gain = gain * one(*cut)
    return gain


def bell_draw(stream_key, extent, scale, reach, cuts=(), held_as=jnp.bfloat16):
    drawn = jax.random.normal(stream_key, extent, jnp.float32) * scale
    if len(cuts) > 0:
        drawn = levels(stream_key, extent, cuts, -0.22, 0.18) * drawn
    return jnp.clip(drawn, min=-reach, max=reach).astype(held_as)


def setup_inputs(seed: int = 0) -> dict:
    streams_of = jax.random.split(jax.random.key(seed), 10)
    return {
        "child_block": bell_draw(streams_of[0], (2, GRID, GRID, TILE, GRID, GRID, TILE), 1.0, 6.0, ((0, 2), (2, 4), (5, 4))),
        "child_row": bell_draw(streams_of[1], (2, TILE, GRID, GRID, TILE), 1.0, 6.0, ((0, 2), (1, 4), (3, 4))),
        "child_col": bell_draw(streams_of[2], (2, TILE, GRID, GRID, TILE), TILE ** -0.5, 0.375, ((0, 2), (1, 4), (3, 4))),
        "child_pivot_inv": bell_draw(streams_of[3], (2, TILE, TILE), TILE ** -0.5, 0.375, ((0, 2),)),
        "child_map": draw_child_map(jax.random.fold_in(streams_of[9], 71), 0),
        "parent_row": bell_draw(streams_of[5], (TILE, GRID, 2 * GRID, TILE), 1.0, 6.0, ((0, 4), (2, 8))),
        "parent_col": bell_draw(streams_of[6], (TILE, 2 * GRID, GRID, TILE), TILE ** -0.5, 0.375, ((0, 8), (2, 4))),
        "parent_pivot_inv": bell_draw(streams_of[7], (TILE, TILE), TILE ** -0.5, 0.375),
        "parent_diag": jnp.clip(1.0 + 2.0 * jax.random.uniform(streams_of[8], (2 * GRID, GRID, TILE), jnp.float32) ** levels(streams_of[8], (2 * GRID, GRID, TILE), ((1, 4),), -0.2, 0.2), 1.0, 3.0),
    }


def inverse_maps(child_map):
    targets = jnp.arange(PARENT_TILES, dtype=jnp.int32)
    matches = child_map[:, None, :] == targets[None, :, None]
    covered = jnp.any(matches, axis=2)
    positions = jnp.arange(CB_TILES, dtype=jnp.int32)
    sources = jnp.sum(jnp.where(matches, positions[None, None, :], 0), axis=2).astype(jnp.int32)
    return covered, sources


def reference(child_block, child_row, child_col, child_pivot_inv, child_map, parent_row, parent_col, parent_pivot_inv, parent_diag):
    contrib = TILE * CB_TILES
    order_total = TILE * PARENT_TILES
    blocks_all = child_block.reshape(2, contrib, contrib)
    cols_all = child_col.reshape(2, TILE, contrib)
    scaled_rows = jnp.stack([jnp.dot(child_pivot_inv[sibling], child_row[sibling].reshape(TILE, contrib), preferred_element_type=jnp.float32) for sibling in range(2)]).astype(jnp.bfloat16)
    parent_scaled = jnp.dot(parent_pivot_inv, parent_row.reshape(TILE, order_total), preferred_element_type=jnp.float32).astype(jnp.bfloat16)
    parent_cols = parent_col.reshape(TILE, order_total)
    diagonal = parent_diag.reshape(order_total)
    covered, sources = inverse_maps(child_map)
    identity = jnp.eye(TILE, dtype=jnp.float32)

    def tile_row(target):
        offset = target * TILE
        panel_cols = lax.dynamic_slice_in_dim(parent_cols, offset, TILE, 1)
        accumulated = -jnp.dot(panel_cols.T, parent_scaled, preferred_element_type=jnp.float32)
        diag_block = identity * lax.dynamic_slice_in_dim(diagonal, offset, TILE, 0)[:, None]
        current = lax.dynamic_slice_in_dim(accumulated, offset, TILE, 1)
        accumulated = lax.dynamic_update_slice_in_dim(accumulated, current + diag_block, offset, 1)
        for sibling in range(2):
            source = sources[sibling, target]
            first_row = source * TILE
            block_rows = lax.dynamic_slice_in_dim(blocks_all[sibling], first_row, TILE, 0)
            panel_child = lax.dynamic_slice_in_dim(cols_all[sibling], first_row, TILE, 1)
            update = jnp.dot(panel_child.T, scaled_rows[sibling], preferred_element_type=jnp.float32)
            contribution = (block_rows.astype(jnp.float32) - update).astype(jnp.bfloat16)
            contribution = lax.optimization_barrier(contribution)
            spread = jnp.zeros((TILE, PARENT_TILES, TILE), jnp.float32).at[:, child_map[sibling], :].set(contribution.reshape(TILE, CB_TILES, TILE).astype(jnp.float32))
            accumulated = accumulated + jnp.where(covered[sibling, target], spread.reshape(TILE, order_total), 0.0)
        return accumulated.astype(jnp.bfloat16)

    result = lax.map(tile_row, jnp.arange(PARENT_TILES, dtype=jnp.int32))
    return result.reshape(2 * GRID, GRID, TILE, GRID, 2 * GRID, TILE)
```

```python
import functools

import jax
import jax.numpy as jnp
from jax import lax
from jax.experimental import pallas as pl
from jax.experimental.pallas import tpu as pltpu
from jax.sharding import PartitionSpec as P

F32 = jnp.float32
BF16 = jnp.bfloat16
PLANE = ("half", "col")


def shifted(value, axis, step):
    count = lax.axis_size(axis)
    return lax.ppermute(value, axis, [(i, (i + step) % count) for i in range(count)])


def gathered(value, axis, order):
    parts = {0: value}
    for step in order:
        parts[step] = shifted(value, axis, step)
    return jnp.concatenate([parts[d] for d in range(lax.axis_size(axis))], axis=1)


def far_first(count):
    return sorted(range(1, count), key=lambda d: -d * (count - d))


def chunks_back(matrix, dim, start, count):
    width = matrix.shape[dim] // count
    return jnp.concatenate(
        [
            lax.dynamic_slice_in_dim(matrix, (start - d) % count * width, width, dim)
            for d in range(count)
        ],
        axis=dim,
    )


def update_kernel(picks, block_ref, col_ref, scaled_ref, out_ref):
    update = lax.dot_general(
        col_ref[0], scaled_ref[0], (((0,), (0,)), ((), ())), preferred_element_type=F32
    )
    out_ref[0] = (block_ref[0, 0].astype(F32) - update).astype(BF16)


def updated_row(block, col, scaled, row_pick, col_picks):
    grid, tile = block.shape[0], block.shape[-1]
    picks = jnp.concatenate([row_pick[None], col_picks])
    spec = pltpu.PrefetchScalarGridSpec(
        num_scalar_prefetch=1,
        grid=(grid,),
        in_specs=[
            pl.BlockSpec((1, 1, tile, tile), lambda s, picks: (picks[0], picks[s + 1], 0, 0)),
            pl.BlockSpec((1, tile, tile), lambda s, picks: (picks[0], 0, 0)),
            pl.BlockSpec((1, tile, tile), lambda s, picks: (picks[s + 1], 0, 0)),
        ],
        out_specs=pl.BlockSpec((1, tile, tile), lambda s, picks: (s, 0, 0)),
    )
    return pl.pallas_call(
        update_kernel,
        grid_spec=spec,
        out_shape=jax.ShapeDtypeStruct((grid, tile, tile), BF16),
        cost_estimate=pl.CostEstimate(
            flops=2 * grid * tile**3, bytes_accessed=7 * grid * tile * tile, transcendentals=0
        ),
        name="child_update",
    )(picks, block, col, scaled)


def front_kernel(grid, picks, *refs):
    arrived = refs[:grid]
    col_ref, scaled_ref, diag_ref, weave_ref, out_ref, held, total, rounded, sems = refs[grid:]
    tile = col_ref.shape[-1]
    step = pl.program_id(0)
    copies = [
        pltpu.make_async_copy(arrived[d], held.at[d], sems.at[d]) for d in range(grid)
    ]

    @pl.when(step == 0)
    def _():
        for copy in copies:
            copy.start()
        for copy in copies:
            copy.wait()

    for q in range(grid):
        base = 2 * grid * q
        value = -lax.dot_general(
            col_ref[0], scaled_ref[q], (((0,), (0,)), ((), ())), preferred_element_type=F32
        )
        for child in range(2):
            chunk = picks[child, step]
            usable = picks[2 + child, step] * picks[6 + child, q]
            source = picks[4 + child, q]
            piece = held[chunk, source]
            value = value + jnp.where(usable > 0, piece.astype(F32), 0.0)
        total[...] = value

        @pl.when(picks[8, q] == step)
        def _():
            rows = lax.broadcasted_iota(jnp.int32, (tile, tile), 0)
            columns = lax.broadcasted_iota(jnp.int32, (tile, tile), 1)
            total[...] += jnp.where(rows == columns, diag_ref[0], 0.0)

        rounded[q] = total[...].astype(BF16)
    rows = tile // grid
    for part in range(grid):
        stacked = jnp.concatenate(
            [rounded[q, part * rows : (part + 1) * rows] for q in range(grid)], axis=0
        )
        woven = jnp.dot(weave_ref[...], stacked, preferred_element_type=F32)
        out_ref[0, part * rows : (part + 1) * rows] = woven.reshape(rows, grid, tile).astype(BF16)


def front(arrived, col, scaled, diag, picks):
    grid, tile = scaled.shape[0], scaled.shape[-1]
    rows = tile // grid
    place = jnp.arange(tile, dtype=jnp.int32)
    weave = (place[None, :] == (place % grid * rows + place // grid)[:, None]).astype(BF16)
    whole = lambda *shape: pl.BlockSpec(shape, lambda s, picks: (0,) * len(shape))
    spec = pltpu.PrefetchScalarGridSpec(
        num_scalar_prefetch=1,
        grid=(2 * grid,),
        in_specs=[pl.BlockSpec(memory_space=pl.ANY)] * grid
        + [
            pl.BlockSpec((1, tile, tile), lambda s, picks: (s, 0, 0)),
            whole(grid, tile, tile),
            pl.BlockSpec((1, 1, tile), lambda s, picks: (s, 0, 0)),
            whole(tile, tile),
        ],
        out_specs=pl.BlockSpec((1, tile, grid, tile), lambda s, picks: (s, 0, 0, 0)),
        scratch_shapes=[
            pltpu.VMEM((grid, 2 * grid, tile, tile), BF16),
            pltpu.VMEM((tile, tile), F32),
            pltpu.VMEM((grid, tile, tile), BF16),
            pltpu.SemaphoreType.DMA((grid,)),
        ],
    )
    return pl.pallas_call(
        functools.partial(front_kernel, grid),
        grid_spec=spec,
        out_shape=jax.ShapeDtypeStruct((2 * grid, tile, grid, tile), BF16),
        compiler_params=pltpu.CompilerParams(vmem_limit_bytes=48 * 2**20),
        cost_estimate=pl.CostEstimate(
            flops=8 * grid * grid * tile**3,
            bytes_accessed=12 * grid * grid * tile * tile,
            transcendentals=0,
        ),
        name="front",
    )(picks, *arrived, col, scaled, diag, weave)


def shards(
    child_block,
    child_row,
    child_col,
    child_pivot_inv,
    child_map,
    parent_row,
    parent_col,
    parent_pivot_inv,
    parent_diag,
):
    grid = lax.axis_size("row")
    tile = child_pivot_inv.shape[-1]
    my_half = lax.axis_index("half")
    my_row = lax.axis_index("row")
    my_col = lax.axis_index("col")
    places = jnp.arange(grid, dtype=jnp.int32)
    shift = child_map[:, ::grid] - 2 * grid * places[None, :]
    unshift = jnp.sum(
        jnp.where(shift[:, None, :] == places[None, :, None], places[None, None, :], 0), axis=2
    )
    mine = jnp.sum(jnp.where(jnp.arange(2)[:, None] == my_half, unshift, 0), axis=0)
    leaving = jnp.sum(
        jnp.where(((places - my_col) % grid)[:, None] == places[None, :], mine[None, :], 0), axis=1
    )

    child_rows = gathered(child_row[0, :, :, 0].transpose(1, 0, 2), "row", far_first(grid))
    child_cols = gathered(child_col[0, :, :, 0].transpose(1, 0, 2), "col", far_first(grid))
    parent_rows = gathered(parent_row[:, :, 0].transpose(1, 0, 2), "row", far_first(grid))
    parent_cols = lax.all_gather(parent_col, PLANE, axis=0, tiled=True)[:, :, 0].transpose(1, 0, 2)
    child_inv = chunks_back(chunks_back(child_pivot_inv[0], 0, my_col, grid), 1, my_row, grid)
    parent_inv = chunks_back(parent_pivot_inv, 1, my_row, grid)
    scale = lambda inverse, rows: jnp.einsum(
        "ab,lbj->laj", inverse, rows, preferred_element_type=F32
    ).astype(BF16)
    child_scaled = scale(child_inv, child_rows)

    blocks = child_block[0, :, 0, :, :, 0].transpose(0, 2, 1, 3)
    arrived = {}
    for step in (*far_first(grid), 0):
        row = updated_row(blocks, child_cols, child_scaled, mine[step], leaving)
        arrived[step] = shifted(row, "row", step) if step else row
    for step in (0, *far_first(grid)):
        row = arrived[step]
        arrived[step] = lax.all_to_all(
            jnp.concatenate([row, row]), PLANE, split_axis=0, concat_axis=0, tiled=True
        )
    parent_scaled = scale(parent_inv, parent_rows)

    targets = jnp.arange(2 * grid, dtype=jnp.int32)
    row_shift = jnp.repeat(shift, 2, axis=1)
    row_usable = (my_row < row_shift) == (targets % 2 == 1)[None, :]
    source = (my_col - shift) % grid + grid * jnp.arange(2, dtype=jnp.int32)[:, None]
    col_usable = (my_col < shift) == (my_half == 1)
    on_diagonal = jnp.where(my_row == my_col, 2 * places + my_half, -1)
    wide = lambda a: jnp.pad(a.astype(jnp.int32), ((0, 0), (0, 2 * grid - a.shape[1])))
    picks = jnp.concatenate(
        [row_shift, row_usable.astype(jnp.int32), wide(source), wide(col_usable), wide(on_diagonal[None])]
    )
    return front(
        [arrived[d] for d in range(grid)], parent_cols, parent_scaled, parent_diag, picks
    ).reshape(2 * grid, 1, tile, grid, 1, tile)


def solution(mesh):
    return jax.shard_map(
        shards,
        mesh=mesh,
        in_specs=(
            P("half", None, "row", None, None, "col", None),
            P("half", "row", None, "col", None),
            P("half", "col", None, "row", None),
            P("half", None, None),
            P(),
            P("row", None, ("half", "col"), None),
            P(("half", "col"), None, "row", None),
            P(),
            P(None, "row", None),
        ),
        out_specs=P(None, "row", None, None, ("half", "col"), None),
        check_vma=False,
    )
```

```python
import functools

import jax
import jax.numpy as jnp
from jax import lax
from jax.experimental import pallas as pl
from jax.experimental.pallas import tpu as pltpu
from jax.sharding import PartitionSpec as P

F32 = jnp.float32
BF16 = jnp.bfloat16
PLANE = ("half", "col")
TRANSPOSED = (((0,), (0,)), ((), ()))


def after(value, *others):
    return lax.optimization_barrier((value, *others))[0]


def shifted(value, axis, step):
    count = lax.axis_size(axis)
    return lax.ppermute(value, axis, [(i, (i + step) % count) for i in range(count)])


def far_first(count):
    return sorted(range(1, count), key=lambda d: -d * (count - d))


def gathered(value, axis):
    count = lax.axis_size(axis)
    parts = {0: value, **{d: shifted(value, axis, d) for d in far_first(count)}}
    return [parts[d] for d in range(count)]


def chunks_of(matrix, dim, order):
    width = matrix.shape[dim] // len(order)
    return jnp.concatenate(
        [lax.dynamic_slice_in_dim(matrix, i * width, width, dim) for i in order], axis=dim
    )


def scaled_rows(inverse, parts, scaled):
    tile = inverse.shape[0]
    for l in range(parts[0].shape[0]):
        rows = jnp.concatenate([part[l] for part in parts], axis=0)
        scaled[:, l * tile : (l + 1) * tile] = jnp.dot(
            inverse, rows, preferred_element_type=F32
        ).astype(BF16)


def update_kernel(grid, picks, *refs):
    block_ref, inverse_ref = refs[:2]
    rows, cols, outs = (refs[2 + grid * i : 2 + grid * (i + 1)] for i in range(3))
    scaled = refs[-1]
    tile = inverse_ref.shape[0]
    scaled_rows(inverse_ref[...], rows, scaled)
    for d in range(grid):
        k = picks[0, d]
        col = jnp.concatenate([part[k] for part in cols], axis=0)
        update = lax.dot_general(col, scaled[...], TRANSPOSED, preferred_element_type=F32)
        for l in range(grid):
            value = block_ref[k, l].astype(F32) - update[:, l * tile : (l + 1) * tile]
            outs[d][picks[1, l]] = value.astype(BF16)


def contribution(block, inverse, rows, cols, picks):
    grid, tile = block.shape[0], block.shape[-1]
    vmem = pl.BlockSpec(memory_space=pltpu.VMEM)
    return pl.pallas_call(
        functools.partial(update_kernel, grid),
        in_specs=[pl.BlockSpec(memory_space=pltpu.SMEM)] + [vmem] * (2 + 2 * grid),
        out_specs=[vmem] * grid,
        out_shape=[jax.ShapeDtypeStruct((grid, tile, tile), BF16)] * grid,
        scratch_shapes=[pltpu.VMEM((tile, grid * tile), BF16)],
        compiler_params=pltpu.CompilerParams(vmem_limit_bytes=56 * 2**20),
        cost_estimate=pl.CostEstimate(
            flops=2 * grid * (grid + 1) * tile**3,
            bytes_accessed=4 * grid * (grid + 1) * tile * tile,
            transcendentals=0,
        ),
        name="child_update",
    )(picks, block, inverse, *rows, *cols)


def front_kernel(grid, picks, *refs):
    arrived, rows, cols = (refs[grid * i : grid * (i + 1)] for i in range(3))
    other_ref, inverse_ref, diag_ref, weave_ref, out_ref = refs[3 * grid : 3 * grid + 5]
    held, scaled, rounded, sems = refs[3 * grid + 5 :]
    tile = inverse_ref.shape[0]
    step = pl.program_id(0)
    copies = [pltpu.make_async_copy(arrived[d], held.at[d], sems.at[d]) for d in range(grid)]

    @pl.when(step == 0)
    def _():
        for copy in copies:
            copy.start()
        scaled_rows(inverse_ref[...], rows, scaled)
        for copy in copies:
            copy.wait()

    col = jnp.concatenate(
        [part[step] for part in cols] + [other_ref[d, step] for d in range(grid)], axis=0
    )
    update = lax.dot_general(col, scaled[...], TRANSPOSED, preferred_element_type=F32)
    chunks = [picks[child, step] for child in range(2)]
    height = tile // grid
    diagonal = lax.broadcasted_iota(jnp.int32, (tile, tile), 0) == lax.broadcasted_iota(
        jnp.int32, (tile, tile), 1
    )
    for q in range(grid):
        value = -update[:, q * tile : (q + 1) * tile]
        for child in range(2):
            usable = picks[2 + child, step] * picks[6 + child, q]
            piece = held[chunks[child], picks[4 + child, q]]
            value = value + jnp.where(usable > 0, piece.astype(F32), 0.0)
        rounded[q] = value.astype(BF16)

        @pl.when(picks[8, q] == step)
        def _():
            rounded[q] = (value + jnp.where(diagonal, diag_ref[0], 0.0)).astype(BF16)

    for part in range(grid):
        stacked = jnp.concatenate(
            [rounded[q, part * height : (part + 1) * height] for q in range(grid)], axis=0
        )
        woven = jnp.dot(weave_ref[...], stacked, preferred_element_type=F32)
        out_ref[0, part * height : (part + 1) * height] = woven.reshape(
            height, grid, tile
        ).astype(BF16)


def front(arrived, rows, cols, other, inverse, diag, picks):
    grid, tile = len(arrived), inverse.shape[0]
    height = tile // grid
    place = jnp.arange(tile, dtype=jnp.int32)
    weave = (place[None, :] == (place % grid * height + place // grid)[:, None]).astype(BF16)
    whole = lambda a: pl.BlockSpec(a.shape, lambda s, picks: (0,) * a.ndim)
    spec = pltpu.PrefetchScalarGridSpec(
        num_scalar_prefetch=1,
        grid=(2 * grid,),
        in_specs=[pl.BlockSpec(memory_space=pl.ANY)] * grid
        + [whole(a) for a in (*rows, *cols, other, inverse)]
        + [pl.BlockSpec((1, 1, tile), lambda s, picks: (s, 0, 0)), whole(weave)],
        out_specs=pl.BlockSpec((1, tile, grid, tile), lambda s, picks: (s, 0, 0, 0)),
        scratch_shapes=[
            pltpu.VMEM((grid, 2 * grid, tile, tile), BF16),
            pltpu.VMEM((tile, grid * tile), BF16),
            pltpu.VMEM((grid, tile, tile), BF16),
            pltpu.SemaphoreType.DMA((grid,)),
        ],
    )
    return pl.pallas_call(
        functools.partial(front_kernel, grid),
        grid_spec=spec,
        out_shape=jax.ShapeDtypeStruct((2 * grid, tile, grid, tile), BF16),
        compiler_params=pltpu.CompilerParams(vmem_limit_bytes=56 * 2**20),
        cost_estimate=pl.CostEstimate(
            flops=8 * grid * grid * tile**3,
            bytes_accessed=12 * grid * grid * tile * tile,
            transcendentals=0,
        ),
        name="front",
    )(picks, *arrived, *rows, *cols, other, inverse, diag, weave)


def shards(
    child_block,
    child_row,
    child_col,
    child_pivot_inv,
    child_map,
    parent_row,
    parent_col,
    parent_pivot_inv,
    parent_diag,
):
    grid = lax.axis_size("row")
    tile = child_pivot_inv.shape[-1]
    my_half = lax.axis_index("half")
    my_row = lax.axis_index("row")
    my_col = lax.axis_index("col")
    places = jnp.arange(grid, dtype=jnp.int32)
    shift = child_map[:, ::grid] - 2 * grid * places[None, :]
    unshift = jnp.sum(
        jnp.where(shift[:, None, :] == places[None, :, None], places[None, None, :], 0), axis=2
    )
    of_mine = lambda pair: jnp.sum(
        jnp.where(jnp.arange(2)[:, None] == my_half, pair, 0), axis=0
    )
    rows_back = [(my_row - d) % grid for d in range(grid)]
    cols_back = [(my_col - d) % grid for d in range(grid)]

    child_rows = gathered(child_row[0, :, :, 0].transpose(1, 0, 2), "row")
    child_cols = gathered(child_col[0, :, :, 0].transpose(1, 0, 2), "col")
    child_inv = chunks_of(chunks_of(child_pivot_inv[0], 0, cols_back), 1, rows_back)
    block_rows = contribution(
        child_block[0, :, 0, :, :, 0].transpose(0, 2, 1, 3),
        child_inv,
        child_rows,
        child_cols,
        jnp.stack([of_mine(unshift), (my_col + of_mine(shift)) % grid]),
    )

    arrived = {d: shifted(block_rows[d], "row", d) for d in range(1, grid)}
    arrived[0] = block_rows[0]

    parent_rows, parent_cols = after(
        (parent_row[:, :, 0].transpose(1, 0, 2), parent_col[:, :, 0].transpose(1, 0, 2)),
        block_rows[0],
    )
    parent_rows = gathered(parent_rows, "row")
    parent_cols = gathered(parent_cols, "col")
    other_cols = lax.ppermute(jnp.stack(parent_cols), "half", [(0, 1), (1, 0)])
    halves = [(my_half + e) % 2 for e in range(2)]
    parent_inv = chunks_of(
        chunks_of(parent_pivot_inv, 0, [h * grid + c for h in halves for c in cols_back]),
        1,
        rows_back,
    )

    for step in range(grid):
        row = arrived[step]
        arrived[step] = lax.all_to_all(
            jnp.concatenate([row, row]), PLANE, split_axis=0, concat_axis=0, tiled=True
        )

    targets = jnp.arange(2 * grid, dtype=jnp.int32)
    row_shift = jnp.repeat(shift, 2, axis=1)
    row_usable = (my_row < row_shift) == (targets % 2 == 1)[None, :]
    source = (my_col - shift) % grid + grid * jnp.arange(2, dtype=jnp.int32)[:, None]
    col_usable = (my_col < shift) == (my_half == 1)
    on_diagonal = jnp.where(my_row == my_col, 2 * places + my_half, -1)[None]
    wide = lambda a: jnp.pad(a.astype(jnp.int32), ((0, 0), (0, 2 * grid - a.shape[1])))
    picks = jnp.concatenate(
        [wide(a) for a in (row_shift, row_usable, source, col_usable, on_diagonal)]
    )
    return front(
        [arrived[d] for d in range(grid)],
        parent_rows,
        parent_cols,
        other_cols,
        parent_inv,
        parent_diag,
        picks,
    ).reshape(2 * grid, 1, tile, grid, 1, tile)


def solution(mesh):
    return jax.shard_map(
        shards,
        mesh=mesh,
        in_specs=(
            P("half", None, "row", None, None, "col", None),
            P("half", "row", None, "col", None),
            P("half", "col", None, "row", None),
            P("half", None, None),
            P(),
            P("row", None, ("half", "col"), None),
            P(("half", "col"), None, "row", None),
            P(),
            P(None, "row", None),
        ),
        out_specs=P(None, "row", None, None, ("half", "col"), None),
        check_vma=False,
    )
```

```python
import functools

import jax
import jax.numpy as jnp
from jax import lax
from jax.experimental import pallas as pl
from jax.experimental.pallas import tpu as pltpu
from jax.sharding import PartitionSpec as P

F32 = jnp.float32
BF16 = jnp.bfloat16
PLANE = ("half", "col")
TRANSPOSED = (((0,), (0,)), ((), ()))


def after(value, *others):
    return lax.optimization_barrier((value, *others))[0]


def shifted(value, axis, step):
    count = lax.axis_size(axis)
    return lax.ppermute(value, axis, [(i, (i + step) % count) for i in range(count)])


def exchanged(value, axis, mask):
    return lax.ppermute(value, axis, [(i, i ^ mask) for i in range(lax.axis_size(axis))])


def far_first(count):
    return sorted(range(1, count), key=lambda d: -d * (count - d))


def gathered(value, axis):
    count = lax.axis_size(axis)
    parts = {0: value, **{d: shifted(value, axis, d) for d in far_first(count)}}
    return [parts[d] for d in range(count)]


def gathered_by_bits(value, axis):
    count = lax.axis_size(axis)
    parts = {0: value}
    mask = count // 2
    while mask:
        parts.update({e ^ mask: exchanged(part, axis, mask) for e, part in parts.items()})
        mask //= 2
    return [parts[e] for e in range(count)]


def reordered(matrix, row_chunks, col_chunks):
    size = matrix.shape[0]
    place = jnp.arange(size, dtype=jnp.int32)

    def chooser(chunks):
        width = size // len(chunks)
        wanted = (jnp.stack(chunks)[:, None] * width + jnp.arange(width)).reshape(size, 1)
        return (wanted == place).astype(BF16)

    if row_chunks is not None:
        matrix = jnp.dot(chooser(row_chunks), matrix)
    return jnp.dot(matrix, chooser(col_chunks).T)


def scaled_rows(inverse, parts, scaled):
    tile = inverse.shape[0]
    for l in range(parts[0].shape[0]):
        rows = jnp.concatenate([part[l] for part in parts], axis=0)
        scaled[:, l * tile : (l + 1) * tile] = jnp.dot(
            inverse, rows, preferred_element_type=F32
        ).astype(BF16)


def update_kernel(grid, picks, *refs):
    block_ref, inverse_ref = refs[:2]
    rows, cols, outs = (refs[2 + grid * i : 2 + grid * (i + 1)] for i in range(3))
    scaled = refs[-1]
    tile = inverse_ref.shape[0]
    width = tile // grid
    scaled_rows(inverse_ref[...], rows, scaled)
    for d in range(grid):
        k = picks[0, d]
        start = pl.multiple_of(k * width, width)
        col = jnp.concatenate([part[pl.ds(start, width)] for part in cols], axis=0)
        update = lax.dot_general(col, scaled[...], TRANSPOSED, preferred_element_type=F32)
        for l in range(grid):
            value = block_ref[k, l].astype(F32) - update[:, l * tile : (l + 1) * tile]
            value = value.astype(BF16)
            outs[d][picks[1, l]] = value
            if d == 0:
                outs[d][grid + picks[1, l]] = value


def contribution(block, inverse, rows, cols, picks):
    grid, tile = block.shape[0], block.shape[-1]
    vmem = pl.BlockSpec(memory_space=pltpu.VMEM)
    return pl.pallas_call(
        functools.partial(update_kernel, grid),
        in_specs=[pl.BlockSpec(memory_space=pltpu.SMEM)] + [vmem] * (2 + 2 * grid),
        out_specs=[vmem] * grid,
        out_shape=[
            jax.ShapeDtypeStruct((grid if d else 2 * grid, tile, tile), BF16) for d in range(grid)
        ],
        scratch_shapes=[pltpu.VMEM((tile, grid * tile), BF16)],
        compiler_params=pltpu.CompilerParams(vmem_limit_bytes=56 * 2**20),
        cost_estimate=pl.CostEstimate(
            flops=2 * grid * (grid + 1) * tile**3,
            bytes_accessed=4 * grid * (grid + 1) * tile * tile,
            transcendentals=0,
        ),
        name="child_update",
    )(picks, block, inverse, *rows, *cols)


def panels_kernel(grid, inverse_ref, *refs):
    rows, cols = refs[:grid], refs[grid : 2 * grid]
    other_ref, scaled, turned = refs[2 * grid :]
    tile = inverse_ref.shape[0]
    width = tile // (2 * grid)
    scaled_rows(inverse_ref[...], rows, scaled)
    for k in range(2 * grid):
        here = slice(tile + k * width, tile + (k + 1) * width)
        there = slice(k * width, (k + 1) * width)
        col = [part[here] for part in cols] + [other_ref[e, there] for e in range(grid)]
        turned[k] = jnp.concatenate(col, axis=0).T


def panels(inverse, rows, cols, other):
    grid, tile = len(rows), inverse.shape[0]
    vmem = pl.BlockSpec(memory_space=pltpu.VMEM)
    return pl.pallas_call(
        functools.partial(panels_kernel, grid),
        in_specs=[vmem] * (2 + 2 * grid),
        out_specs=[vmem] * 2,
        out_shape=[
            jax.ShapeDtypeStruct((tile, grid * tile), BF16),
            jax.ShapeDtypeStruct((2 * grid, tile, tile), BF16),
        ],
        compiler_params=pltpu.CompilerParams(vmem_limit_bytes=56 * 2**20),
        cost_estimate=pl.CostEstimate(
            flops=2 * grid * tile**3, bytes_accessed=12 * grid * tile * tile, transcendentals=0
        ),
        name="parent_panels",
    )(inverse, *rows, *cols, other)


def front_kernel(where, picks, *refs):
    grid = len(where)
    count = 1 + max(i for i, _ in where)
    arrived = refs[:count]
    col_ref, scaled_ref, diag_ref, weave_ref, out_ref, held, sems = refs[count:]
    tile = weave_ref.shape[0]
    step = pl.program_id(0)
    copies = [
        pltpu.make_async_copy(arrived[i].at[:, j], held.at[d], sems.at[d])
        for d, (i, j) in enumerate(where)
    ]

    @pl.when(step == 0)
    def _():
        for copy in copies:
            copy.start()

    for d in range(grid):

        @pl.when(picks[9, d] == step)
        def _():
            copies[d].wait()

    update = jnp.dot(col_ref[0], scaled_ref[...], preferred_element_type=F32)
    height = tile // grid
    lanes = 128 if height <= 128 else tile
    for part in range(grid):
        rows = slice(part * height, (part + 1) * height)
        near = part * height // lanes * lanes
        on = lax.broadcasted_iota(jnp.int32, (height, lanes), 0) + (
            part * height - near
        ) == lax.broadcasted_iota(jnp.int32, (height, lanes), 1)
        stacked = []
        for q in range(grid):
            value = -update[rows, q * tile : (q + 1) * tile]
            for child in range(2):
                usable = picks[2 + child, step] * picks[6 + child, q]
                piece = held[picks[child, step], picks[4 + child, q], rows]
                value = value + jnp.where(usable > 0, piece.astype(F32), 0.0)
            entries = jnp.where(picks[8, q] == step, diag_ref[0, :, near : near + lanes], 0.0)
            bands = [value[:, at : at + lanes] for at in range(0, tile, lanes)]
            bands[near // lanes] += jnp.where(on, entries, 0.0)
            stacked.append(jnp.concatenate(bands, axis=1).astype(BF16))
        woven = jnp.dot(
            weave_ref[...], jnp.concatenate(stacked, axis=0), preferred_element_type=F32
        )
        out_ref[0, rows] = woven.reshape(height, grid, tile).astype(BF16)


def front(arrived, where, col, scaled, diag, picks):
    grid, tile = len(where), col.shape[-1]
    height = tile // grid
    place = jnp.arange(tile, dtype=jnp.int32)
    weave = (place[None, :] == (place % grid * height + place // grid)[:, None]).astype(BF16)
    spec = pltpu.PrefetchScalarGridSpec(
        num_scalar_prefetch=1,
        grid=(2 * grid,),
        in_specs=[pl.BlockSpec(memory_space=pl.ANY)] * len(arrived)
        + [
            pl.BlockSpec((1, tile, tile), lambda s, picks: (s, 0, 0)),
            pl.BlockSpec((tile, grid * tile), lambda s, picks: (0, 0)),
            pl.BlockSpec((1, 1, tile), lambda s, picks: (s, 0, 0)),
            pl.BlockSpec((tile, tile), lambda s, picks: (0, 0)),
        ],
        out_specs=pl.BlockSpec((1, tile, grid, tile), lambda s, picks: (s, 0, 0, 0)),
        scratch_shapes=[
            pltpu.VMEM((grid, 2 * grid, tile, tile), BF16),
            pltpu.SemaphoreType.DMA((grid,)),
        ],
    )
    return pl.pallas_call(
        functools.partial(front_kernel, where),
        grid_spec=spec,
        out_shape=jax.ShapeDtypeStruct((2 * grid, tile, grid, tile), BF16),
        compiler_params=pltpu.CompilerParams(vmem_limit_bytes=56 * 2**20),
        cost_estimate=pl.CostEstimate(
            flops=8 * grid * grid * tile**3,
            bytes_accessed=12 * grid * grid * tile * tile,
            transcendentals=0,
        ),
        name="front",
    )(picks, *arrived, col, scaled, diag, weave)


def to_plane(*block_rows):
    return lax.all_to_all(
        jnp.concatenate([jnp.stack(block_rows, axis=1)] * 2),
        PLANE,
        split_axis=0,
        concat_axis=0,
        tiled=True,
    )


def shards(
    child_block,
    child_row,
    child_col,
    child_pivot_inv,
    child_map,
    parent_row,
    parent_col,
    parent_pivot_inv,
    parent_diag,
):
    grid = lax.axis_size("row")
    tile = child_pivot_inv.shape[-1]
    my_half = lax.axis_index("half")
    my_row = lax.axis_index("row")
    my_col = lax.axis_index("col")
    places = jnp.arange(grid, dtype=jnp.int32)
    shift = child_map[:, ::grid] - 2 * grid * places[None, :]
    unshift = jnp.sum(
        jnp.where(shift[:, None, :] == places[None, :, None], places[None, None, :], 0), axis=2
    )
    of_mine = lambda pair: jnp.sum(
        jnp.where(jnp.arange(2)[:, None] == my_half, pair, 0), axis=0
    )
    row_chunks = [(my_row - d) % grid for d in range(grid)]
    col_chunks = [my_col ^ e for e in range(grid)]
    plane_chunks = [(my_half ^ h) * grid + c for h in range(2) for c in col_chunks]

    child_rows = gathered(child_row[0, :, :, 0].transpose(1, 0, 2), "row")
    cols = gathered_by_bits(
        jnp.concatenate(
            [
                child_col[0, :, :, 0].transpose(1, 0, 2).reshape(tile, tile),
                parent_col[:, :, 0].transpose(1, 0, 2).reshape(tile, tile),
            ]
        ),
        "col",
    )
    other_cols = exchanged(jnp.stack([part[tile:] for part in cols]), "half", 1)
    block_rows = contribution(
        child_block[0, :, 0, :, :, 0].transpose(0, 2, 1, 3),
        reordered(child_pivot_inv[0], col_chunks, row_chunks),
        child_rows,
        cols,
        jnp.stack([of_mine(unshift), (my_col + of_mine(shift)) % grid]),
    )

    far = grid // 2
    first = [d for d in range(1, grid) if d != far]
    moved = lax.optimization_barrier([shifted(block_rows[d], "row", d) for d in first])
    staying = lax.all_to_all(
        block_rows[0][:, None], PLANE, split_axis=0, concat_axis=0, tiled=True
    )
    last = shifted(after(block_rows[far], moved), "row", far)
    middle = to_plane(*after(moved, other_cols, staying))
    parent_rows = gathered(after(parent_row[:, :, 0].transpose(1, 0, 2), last), "row")
    ending = to_plane(after(last, middle))
    scaled, turned = panels(
        reordered(parent_pivot_inv, plane_chunks, row_chunks), parent_rows, cols, other_cols
    )
    where = {0: (0, 0), far: (2, 0), **{d: (1, i) for i, d in enumerate(first)}}

    targets = jnp.arange(2 * grid, dtype=jnp.int32)
    row_shift = jnp.repeat(shift, 2, axis=1)
    row_usable = (my_row < row_shift) == (targets % 2 == 1)[None, :]
    source = (my_col - shift) % grid + grid * jnp.arange(2, dtype=jnp.int32)[:, None]
    col_usable = (my_col < shift) == (my_half == 1)
    on_diagonal = jnp.where(my_row == my_col, 2 * places + my_half, -1)[None]
    first_used = 2 * jnp.min(unshift, axis=0)[None]
    wide = lambda a: jnp.pad(a.astype(jnp.int32), ((0, 0), (0, 2 * grid - a.shape[1])))
    picks = jnp.concatenate(
        [wide(a) for a in (row_shift, row_usable, source, col_usable, on_diagonal, first_used)]
    )
    return front(
        [staying, middle, ending],
        [where[d] for d in range(grid)],
        turned,
        scaled,
        parent_diag,
        picks,
    ).reshape(2 * grid, 1, tile, grid, 1, tile)


def solution(mesh):
    return jax.shard_map(
        shards,
        mesh=mesh,
        in_specs=(
            P("half", None, "row", None, None, "col", None),
            P("half", "row", None, "col", None),
            P("half", "col", None, "row", None),
            P("half", None, None),
            P(),
            P("row", None, ("half", "col"), None),
            P(("half", "col"), None, "row", None),
            P(),
            P(None, "row", None),
        ),
        out_specs=P(None, "row", None, None, ("half", "col"), None),
        check_vma=False,
    )
```

```python
import functools

import jax
import jax.numpy as jnp
from jax import lax
from jax.experimental import pallas as pl
from jax.experimental.pallas import tpu as pltpu
from jax.sharding import PartitionSpec as P

F32 = jnp.float32
BF16 = jnp.bfloat16
PLANE = ("half", "col")
TRANSPOSED = (((0,), (0,)), ((), ()))


def after(value, *others):
    return lax.optimization_barrier((value, *others))[0]


def shifted(value, axis, step):
    count = lax.axis_size(axis)
    return lax.ppermute(value, axis, [(i, (i + step) % count) for i in range(count)])


def exchanged(value, axis, mask):
    return lax.ppermute(value, axis, [(i, i ^ mask) for i in range(lax.axis_size(axis))])


def far_first(count):
    return sorted(range(1, count), key=lambda d: -d * (count - d))


def gathered(value, axis):
    count = lax.axis_size(axis)
    parts = {0: value, **{d: shifted(value, axis, d) for d in far_first(count)}}
    return [parts[d] for d in range(count)]


def gathered_by_bits(value, axis, meanwhile):
    count = lax.axis_size(axis)
    parts = {0: value}
    mask = count // 2
    while mask:
        sent = {**parts, 0: value if mask > 1 else after(value, meanwhile)}
        parts.update({e ^ mask: exchanged(part, axis, mask) for e, part in sent.items()})
        mask //= 2
    return [parts[e] for e in range(count)]


def reordered(matrix, row_chunks, col_chunks):
    size = matrix.shape[0]
    place = jnp.arange(size, dtype=jnp.int32)

    def chooser(chunks):
        width = size // len(chunks)
        wanted = (jnp.stack(chunks)[:, None] * width + jnp.arange(width)).reshape(size, 1)
        return (wanted == place).astype(BF16)

    matrix = jnp.dot(chooser(row_chunks), matrix)
    return matrix if col_chunks is None else jnp.dot(matrix, chooser(col_chunks).T)


def scaled_rows(inverse, parts, scaled):
    tile = inverse.shape[0]
    for l in range(parts[0].shape[0]):
        rows = jnp.concatenate([part[l] for part in parts], axis=0)
        scaled[:, l * tile : (l + 1) * tile] = jnp.dot(
            inverse, rows, preferred_element_type=F32
        ).astype(BF16)


def update_kernel(grid, picks, *refs):
    block_ref, inverse_ref = refs[:2]
    rows, cols, outs = (refs[2 + grid * i : 2 + grid * (i + 1)] for i in range(3))
    scaled = refs[-1]
    tile = inverse_ref.shape[0]
    width = tile // grid
    scaled_rows(inverse_ref[...], rows, scaled)
    for d in range(grid):
        k = picks[0, d]
        start = pl.multiple_of(k * width, width)
        col = jnp.concatenate([part[pl.ds(start, width)] for part in cols], axis=0)
        update = lax.dot_general(col, scaled[...], TRANSPOSED, preferred_element_type=F32)
        for l in range(grid):
            value = block_ref[k, l].astype(F32) - update[:, l * tile : (l + 1) * tile]
            value = value.astype(BF16)
            outs[d][picks[1, l]] = value
            if d == 0:
                outs[d][grid + picks[1, l]] = value


def contribution(block, inverse, rows, cols, picks):
    grid, tile = block.shape[0], block.shape[-1]
    vmem = pl.BlockSpec(memory_space=pltpu.VMEM)
    return pl.pallas_call(
        functools.partial(update_kernel, grid),
        in_specs=[pl.BlockSpec(memory_space=pltpu.SMEM)] + [vmem] * (2 + 2 * grid),
        out_specs=[vmem] * grid,
        out_shape=[
            jax.ShapeDtypeStruct((grid if d else 2 * grid, tile, tile), BF16) for d in range(grid)
        ],
        scratch_shapes=[pltpu.VMEM((tile, grid * tile), BF16)],
        compiler_params=pltpu.CompilerParams(vmem_limit_bytes=56 * 2**20),
        cost_estimate=pl.CostEstimate(
            flops=2 * grid * (grid + 1) * tile**3,
            bytes_accessed=4 * grid * (grid + 1) * tile * tile,
            transcendentals=0,
        ),
        name="child_update",
    )(picks, block, inverse, *rows, *cols)


def panels_kernel(grid, inverse_ref, rows_ref, *refs):
    cols = refs[:grid]
    other_ref, scaled, turned = refs[grid:]
    tile = inverse_ref.shape[0]
    width = tile // (2 * grid)
    scaled_rows(inverse_ref[...], [rows_ref], scaled)
    for k in range(2 * grid):
        here = slice(tile + k * width, tile + (k + 1) * width)
        there = slice(k * width, (k + 1) * width)
        col = [part[here] for part in cols] + [other_ref[e, there] for e in range(grid)]
        turned[k] = jnp.concatenate(col, axis=0).T


def panels(inverse, rows, cols, other):
    grid, tile = len(cols), inverse.shape[0]
    vmem = pl.BlockSpec(memory_space=pltpu.VMEM)
    return pl.pallas_call(
        functools.partial(panels_kernel, grid),
        in_specs=[vmem] * (3 + grid),
        out_specs=[vmem] * 2,
        out_shape=[
            jax.ShapeDtypeStruct((tile, grid * tile), BF16),
            jax.ShapeDtypeStruct((2 * grid, tile, tile), BF16),
        ],
        compiler_params=pltpu.CompilerParams(vmem_limit_bytes=56 * 2**20),
        cost_estimate=pl.CostEstimate(
            flops=2 * grid * tile**3, bytes_accessed=12 * grid * tile * tile, transcendentals=0
        ),
        name="parent_panels",
    )(inverse, rows, *cols, other)


def front_kernel(where, count, picks, *refs):
    arrived = refs[:count]
    col_ref, scaled_ref, diag_ref, weave_ref = refs[count : count + 4]
    out_ref, held, sems = refs[-3:]
    tile = weave_ref.shape[0]
    grid = held.shape[2]
    step = pl.program_id(0)
    here = picks[0, step]
    slot = lax.rem(step, 2)

    def pieces(place, child, slot):
        i, j = place
        return pltpu.make_async_copy(
            arrived[i].at[child * grid : (child + 1) * grid, j],
            held.at[slot, child],
            sems.at[slot, child],
        )

    def fetch(at, slot):
        for child in range(2):
            wanted = picks[1 + child, picks[0, at]]
            for d, place in where.items():

                @pl.when(wanted == d)
                def _():
                    pieces(place, child, slot).start()

    @pl.when(step == 0)
    def _():
        fetch(0, 0)

    @pl.when(step + 1 < pl.num_programs(0))
    def _():
        fetch(step + 1, 1 - slot)

    update = jnp.dot(col_ref[0], scaled_ref[...], preferred_element_type=F32)
    for child in range(2):
        pieces((0, 0), child, slot).wait()
    height = tile // grid
    lanes = 128 if height <= 128 else tile
    for part in range(grid):
        rows = slice(part * height, (part + 1) * height)
        near = part * height // lanes * lanes
        on = lax.broadcasted_iota(jnp.int32, (height, lanes), 0) + (
            part * height - near
        ) == lax.broadcasted_iota(jnp.int32, (height, lanes), 1)
        stacked = []
        for q in range(grid):
            value = -update[rows, q * tile : (q + 1) * tile]
            for child in range(2):
                usable = picks[3 + child, here] * picks[7 + child, q]
                piece = held[slot, child, picks[5 + child, q], rows]
                value = value + jnp.where(usable > 0, piece.astype(F32), 0.0)
            entries = jnp.where(picks[9, q] == here, diag_ref[0, :, near : near + lanes], 0.0)
            bands = [value[:, at : at + lanes] for at in range(0, tile, lanes)]
            bands[near // lanes] += jnp.where(on, entries, 0.0)
            stacked.append(jnp.concatenate(bands, axis=1).astype(BF16))
        woven = jnp.dot(
            weave_ref[...], jnp.concatenate(stacked, axis=0), preferred_element_type=F32
        )
        out_ref[0, rows] = woven.reshape(height, grid, tile).astype(BF16)


def front(arrived, where, steps, col, scaled, diag, picks, begun=None):
    tile = col.shape[-1]
    grid = scaled.shape[-1] // tile
    height = tile // grid
    place = jnp.arange(tile, dtype=jnp.int32)
    weave = (place[None, :] == (place % grid * height + place // grid)[:, None]).astype(BF16)
    hbm = pl.BlockSpec(memory_space=pl.ANY)
    operands = [*arrived, col, scaled, diag, weave]
    in_specs = [hbm] * len(arrived) + [
        pl.BlockSpec((1, tile, tile), lambda s, picks: (picks[0, s], 0, 0)),
        pl.BlockSpec((tile, grid * tile), lambda s, picks: (0, 0)),
        pl.BlockSpec((1, 1, tile), lambda s, picks: (picks[0, s], 0, 0)),
        pl.BlockSpec((tile, tile), lambda s, picks: (0, 0)),
    ]
    aliases = {}
    if begun is not None:
        aliases[1 + len(operands)] = 0
        operands.append(begun)
        in_specs.append(hbm)
    spec = pltpu.PrefetchScalarGridSpec(
        num_scalar_prefetch=1,
        grid=(steps,),
        in_specs=in_specs,
        out_specs=pl.BlockSpec((1, tile, grid, tile), lambda s, picks: (picks[0, s], 0, 0, 0)),
        scratch_shapes=[
            pltpu.VMEM((2, 2, grid, tile, tile), BF16),
            pltpu.SemaphoreType.DMA((2, 2)),
        ],
    )
    return pl.pallas_call(
        functools.partial(front_kernel, where, len(arrived)),
        grid_spec=spec,
        out_shape=jax.ShapeDtypeStruct((2 * grid, tile, grid, tile), BF16),
        input_output_aliases=aliases,
        compiler_params=pltpu.CompilerParams(vmem_limit_bytes=48 * 2**20),
        cost_estimate=pl.CostEstimate(
            flops=4 * steps * grid * tile**3,
            bytes_accessed=6 * steps * grid * tile * tile,
            transcendentals=0,
        ),
        name="front" if begun is None else "front_end",
    )(picks, *operands)


def to_plane(*block_rows):
    return lax.all_to_all(
        jnp.concatenate([jnp.stack(block_rows, axis=1)] * 2),
        PLANE,
        split_axis=0,
        concat_axis=0,
        tiled=True,
    )


def shards(
    child_block,
    child_row,
    child_col,
    child_pivot_inv,
    child_map,
    parent_row,
    parent_col,
    parent_pivot_inv,
    parent_diag,
):
    grid = lax.axis_size("row")
    tile = child_pivot_inv.shape[-1]
    my_half = lax.axis_index("half")
    my_row = lax.axis_index("row")
    my_col = lax.axis_index("col")
    places = jnp.arange(grid, dtype=jnp.int32)
    shift = child_map[:, ::grid] - 2 * grid * places[None, :]
    unshift = jnp.sum(
        jnp.where(shift[:, None, :] == places[None, :, None], places[None, None, :], 0), axis=2
    )
    of_mine = lambda pair: jnp.sum(
        jnp.where(jnp.arange(2)[:, None] == my_half, pair, 0), axis=0
    )
    row_chunks = [(my_row - d) % grid for d in range(grid)]
    col_chunks = [my_col ^ e for e in range(grid)]
    plane_chunks = [(my_half ^ h) * grid + c for h in range(2) for c in col_chunks]

    blocks = child_block[0, :, 0, :, :, 0].transpose(0, 2, 1, 3)
    child_rows = gathered(child_row[0, :, :, 0].transpose(1, 0, 2), "row")
    cols = gathered_by_bits(
        jnp.concatenate(
            [
                child_col[0, :, :, 0].transpose(1, 0, 2).reshape(tile, tile),
                parent_col[:, :, 0].transpose(1, 0, 2).reshape(tile, tile),
            ]
        ),
        "col",
        blocks,
    )
    other_cols = exchanged(jnp.stack([part[tile:] for part in cols]), "half", 1)
    block_rows = contribution(
        blocks,
        reordered(child_pivot_inv[0], col_chunks, row_chunks),
        child_rows,
        cols,
        jnp.stack([of_mine(unshift), (my_col + of_mine(shift)) % grid]),
    )

    far = grid // 2
    first = [d for d in range(1, grid) if d != far]
    moved = lax.optimization_barrier([shifted(block_rows[d], "row", d) for d in first])
    staying = lax.all_to_all(
        block_rows[0][:, None], PLANE, split_axis=0, concat_axis=0, tiled=True
    )
    last = shifted(after(block_rows[far], moved), "row", far)
    middle = to_plane(*after(moved, other_cols, staying))
    parent_rows = lax.all_gather(
        after(parent_row[:, :, 0].transpose(1, 0, 2), moved), "row", axis=1, tiled=True
    )
    ending = to_plane(after(last, middle, parent_rows))
    scaled, turned = panels(
        reordered(parent_pivot_inv, plane_chunks, None), parent_rows, cols, other_cols
    )

    targets = jnp.arange(2 * grid, dtype=jnp.int32)
    row_shift = jnp.repeat(shift, 2, axis=1)
    row_usable = (my_row < row_shift) == (targets % 2 == 1)[None, :]
    row_shift = jnp.where(row_usable, row_shift, 0)
    source = (my_col - shift) % grid
    col_usable = (my_col < shift) == (my_half == 1)
    on_diagonal = jnp.where(my_row == my_col, 2 * places + my_half, -1)[None]
    reached = jnp.any(row_shift == far, axis=0)
    spare = jnp.sum((targets[None, :] <= targets[:, None]) & ~reached[None, :], axis=1)
    early = jnp.minimum(targets, spare[-1] - 1)
    early = jnp.sum(
        jnp.where((spare - 1 == early[:, None]) & ~reached[None, :], targets[None, :], 0), axis=1
    )
    late = jnp.max(jnp.where(row_shift == far, targets[None, :], -1), axis=1)
    wide = lambda a: jnp.pad(a.astype(jnp.int32), ((0, 0), (0, 2 * grid - a.shape[1])))
    picks = [wide(a) for a in (row_shift, row_usable, source, col_usable, on_diagonal)]
    kept = {0: (0, 0), **{d: (1, i) for i, d in enumerate(first)}}
    begun = front(
        [staying, middle],
        kept,
        2 * grid - 1,
        turned,
        scaled,
        parent_diag,
        jnp.concatenate([early[None], *picks]),
    )
    return front(
        [staying, middle, ending],
        {**kept, far: (2, 0)},
        2,
        turned,
        scaled,
        parent_diag,
        jnp.concatenate([wide(late[None]), *picks]),
        begun,
    ).reshape(2 * grid, 1, tile, grid, 1, tile)


def solution(mesh):
    return jax.shard_map(
        shards,
        mesh=mesh,
        in_specs=(
            P("half", None, "row", None, None, "col", None),
            P("half", "row", None, "col", None),
            P("half", "col", None, "row", None),
            P("half", None, None),
            P(),
            P("row", None, ("half", "col"), None),
            P(("half", "col"), None, "row", None),
            P(),
            P(None, "row", None),
        ),
        out_specs=P(None, "row", None, None, ("half", "col"), None),
        check_vma=False,
    )
```
